32 devices in a mesh: parts: 2 (over y), row: 2 (over core), col: 8 (over z, x).
Axes of the slice: x: 2, y: 2, z: 4, core: 2. Of those that a mesh axis runs over, the one named last changes fastest.
Arguments:
- sigma_anc: float32 [24576, 12288], P(('parts', 'col'), 'row'), parts along dimension 0, may hold values from -20 to 20, as said below
- factor_rows: float32 [4, 12288, 512], P('parts', ('row', 'col')), parts along dimension 0, may hold values from -0.0546875 to 0.0546875
- diag_inverse: float32 [4, 512, 512], P('parts'), parts along dimension 0, may hold values from -8 to 8, as said below
- row_pattern: int32 [4, 96], P('parts'), parts along dimension 0, may hold values 0 or 1
- anc_pattern: int32 [192, 96], P('parts'), parts along dimension 0, may hold values 0 or 1
Outputs:
- sigma_cross: float32 [4, 12288, 512], P('parts', 'col'), parts along dimension 0
- sigma_diag: float32 [4, 512, 512], P('parts'), parts along dimension 0
The draws below stay inside these ranges and needn't reach their ends.
There are 2 independent parts, one for each index of `parts`. The reference program is written for one: setup_inputs(seed, part) draws one part's arguments, and reference() takes and returns one part's arrays. A program takes and returns all parts, laid end to end along the dimension named above; each array names one. Nothing has to cross between parts.
Inputs may be any that keep to these rules, and one draw needn't show every extreme that they name: `sigma_anc`: symmetric. `diag_inverse`: each supernode's block is lower triangular.
All inputs are finite; a program needn't handle non-finite values.
Results may differ from the reference program's by a relative error of at most 0.000071.
Values sent between devices are 32-bit elements; how exact they have to be, the bound alone decides.
No kernel may reach another device: no remote copies, remote signals or barrier semaphores. Data moves between devices by JAX's collectives and lax.ppermute only.
A program may use at most 448 MiB of HBM per device.

```python
import math
import jax
import jax.numpy as jnp
from jax import lax

F = 12288
B = 512
S = 2
BLK = 128
NB = 96


def draw_sigma_anc(key, part):
    key = jax.random.fold_in(key, 11)
    first, second = jax.random.split(key)
    noise = jax.random.normal(first, (F, F), jnp.float32)
    scales = jnp.exp(jax.random.uniform(second, (F,), jnp.float32, 0.0, math.log(10.0)))
    spread = jnp.sqrt(scales)
    sym = (noise + noise.T) * (0.35 / math.sqrt(F))
    sym = sym * spread[:, None] * spread[None, :]
    eye = jnp.eye(F, dtype=jnp.float32)
    return sym * (1.0 - eye) + eye * scales[None, :]


def draw_diag_inverse(key, part):
    key = jax.random.fold_in(key, 23)
    first, second = jax.random.split(key)
    noise = jax.random.normal(first, (S, B, B), jnp.float32)
    diagonal = jnp.exp(jax.random.uniform(second, (S, B), jnp.float32, 0.0, math.log(8.0)))
    strict = jnp.tril(noise * (0.5 / math.sqrt(B)), -1)
    eye = jnp.eye(B, dtype=jnp.float32)
    return strict + eye[None, :, :] * diagonal[:, None, :]


def plant(entries, stream_key, low, high):
    spot = [jax.random.randint(jax.random.fold_in(stream_key, axis), (), 0, length) for axis, length in enumerate(entries.shape)]
    longest = entries.shape.index(max(entries.shape))
    neighbour = spot[:longest] + [(spot[longest] + 1) % entries.shape[longest]] + spot[longest + 1:]
    return entries.at[tuple(spot)].set(low).at[tuple(neighbour)].set(high)


def level_of(rng, shape, cuts, low, largest):
    loudness, own = 1.0, jax.random.fold_in(rng, 6)
    for axis_at, parts in cuts:
        steps = jnp.exp(jax.random.uniform(jax.random.fold_in(own, axis_at), (parts,), jnp.float32, low / len(cuts), largest / len(cuts)))
        loudness = loudness * jnp.repeat(steps, shape[axis_at] // parts).reshape([-1 if axis == axis_at else 1 for axis in range(len(shape))])
    return loudness


def normal_values(own_key, extent, deviation, limit, shards=(), kind=jnp.bfloat16):
    values = deviation * jax.random.normal(own_key, extent, jnp.float32)
    if shards:
        values = values * level_of(own_key, extent, shards, -0.22, 0.18)
    return jnp.clip(values, -limit, limit).astype(kind)


def setup_inputs(seed: int = 0, part: int = 0) -> dict:
    arg_keys = jax.random.split(jax.random.key(seed), 6)
    part_splits = jax.random.split(jax.random.fold_in(arg_keys[5], part), 6)
    sigma_anc = draw_sigma_anc(jax.random.fold_in(jax.random.fold_in(arg_keys[5], part), 71), part)
    factor_rows = normal_values(part_splits[1], (S, F, B), F ** -0.5, 0.0546875, ((1, 16),), jnp.float32)
    diag_inverse = draw_diag_inverse(jax.random.fold_in(jax.random.fold_in(arg_keys[5], part), 71), part)
    row_pattern = plant((jax.random.randint(part_splits[3], (S, NB), 0, 8) < 7).astype(jnp.int32), jax.random.fold_in(part_splits[3], 1), 0, 1)
    anc_pattern = plant((jax.random.randint(part_splits[4], (NB, NB), 0, 4) < 3).astype(jnp.int32), jax.random.fold_in(part_splits[4], 1), 0, 1)
    return {"sigma_anc": sigma_anc, "factor_rows": factor_rows, "diag_inverse": diag_inverse, "row_pattern": row_pattern, "anc_pattern": anc_pattern}


def reference(sigma_anc, factor_rows, diag_inverse, row_pattern, anc_pattern):
    high = lax.Precision.HIGHEST
    row_mask = jnp.repeat(row_pattern.astype(jnp.float32), BLK, axis=1)
    lower = factor_rows * row_mask[:, :, None]
    block_mask = jnp.repeat(jnp.repeat(anc_pattern.astype(jnp.float32), BLK, axis=0), BLK, axis=1)
    kept = sigma_anc * block_mask
    scaled = jnp.einsum("sfb,sbc->sfc", lower, diag_inverse, precision=high)

    def one_node(u_block):
        return -jnp.dot(kept, u_block, precision=high, preferred_element_type=jnp.float32)

    sigma_cross = lax.map(one_node, scaled)
    square = jnp.einsum("sbc,sbd->scd", diag_inverse, diag_inverse, precision=high)
    correction = jnp.einsum("sfc,sfd->scd", scaled, sigma_cross, precision=high)
    sigma_diag = square - correction
    return sigma_cross, sigma_diag
```

```python
import functools

import jax
import jax.numpy as jnp
from jax import lax
from jax.experimental import pallas as pl
from jax.experimental.pallas import tpu as pltpu
from jax.sharding import PartitionSpec as P

BLK = 128
HIGH = lax.Precision.HIGH
HIGHEST = lax.Precision.HIGHEST


def _accumulate_body(n, row_step, ncols_blk, has_acc, tab, mask, *refs):
    pieces, refs = refs[:n], refs[n:]
    a_ref = refs[0]
    acc_ref = refs[1] if has_acc else None
    out_ref, u_ref = refs[-2:]
    depth = pieces[0].shape[0]
    t = pl.program_id(0)

    @pl.when(t == 0)
    def _():
        if has_acc:
            out_ref[...] = acc_ref[...]
        else:
            out_ref[...] = jnp.zeros_like(out_ref)

    for k, piece in enumerate(pieces):

        @pl.when(t == k)
        def _(piece=piece):
            v = piece[...]
            hi = v.astype(jnp.bfloat16)
            u_ref[0:depth, :] = hi
            u_ref[depth : 2 * depth, :] = (v - hi.astype(jnp.float32)).astype(jnp.bfloat16)
            u_ref[2 * depth : 3 * depth, :] = hi

    per = depth // BLK
    col0 = tab[t] * per
    lane = lax.broadcasted_iota(jnp.int32, (1, depth), 1) // BLK
    for m in range(a_ref.shape[0] // row_step):
        rows = []
        for b in range(row_step // BLK):
            blk = m * (row_step // BLK) + b
            keep = jnp.zeros((1, depth), jnp.float32)
            for j in range(per):
                kept = mask[blk * ncols_blk + col0 + j].astype(jnp.float32)
                keep = jnp.where(lane == j, kept, keep)
            rows.append(a_ref[blk * BLK : (blk + 1) * BLK, :] * keep)
        a = jnp.concatenate(rows, axis=0)
        hi = a.astype(jnp.bfloat16)
        lo = (a - hi.astype(jnp.float32)).astype(jnp.bfloat16)
        lhs = jnp.concatenate([hi, hi, lo], axis=1)
        at = slice(m * row_step, (m + 1) * row_step)
        out_ref[at, :] += jnp.dot(lhs, u_ref[...], preferred_element_type=jnp.float32)


def accumulate(acc, sigma, mask, table, pieces):
    nrows, ncols = sigma.shape
    depth, width = pieces[0].shape
    n = len(pieces)
    row_step = next(s for s in (512, 256, 128) if nrows % s == 0)
    whole = lambda shape: pl.BlockSpec(shape, lambda t, *_: (0, 0), pipeline_mode=pl.Buffered(1))
    in_specs = [whole(p.shape) for p in pieces]
    in_specs.append(pl.BlockSpec((nrows, depth), lambda t, tab, mask: (0, tab[t])))
    args = [*pieces, sigma]
    if acc is not None:
        in_specs.append(whole(acc.shape))
        args.append(acc)
    return pl.pallas_call(
        functools.partial(_accumulate_body, n, row_step, ncols // BLK, acc is not None),
        grid_spec=pltpu.PrefetchScalarGridSpec(
            num_scalar_prefetch=2,
            grid=(n,),
            in_specs=in_specs,
            out_specs=whole((nrows, width)),
            scratch_shapes=[pltpu.VMEM((3 * depth, width), jnp.bfloat16)],
        ),
        out_shape=jax.ShapeDtypeStruct((nrows, width), jnp.float32),
        compiler_params=pltpu.CompilerParams(
            dimension_semantics=("arbitrary",), vmem_limit_bytes=48 * 2**20
        ),
        cost_estimate=pl.CostEstimate(
            flops=6 * n * depth * nrows * width,
            bytes_accessed=4 * (n * depth * nrows + n * depth * width + 2 * nrows * width),
            transcendentals=0,
        ),
    )(jnp.stack(table), mask, *args)


def _negate_body(acc_ref, got_ref, *refs):
    refs[-1][0] = -(acc_ref[...] + got_ref[...])


def negate_into(full, acc, got, shape, s, at):
    nrows, width = acc.shape
    step = nrows // 3
    tile = pl.BlockSpec((step, width), lambda i: (i, 0))
    in_specs, args, aliases = [tile, tile], [acc, got], {}
    if full is not None:
        in_specs.append(pl.BlockSpec(memory_space=pl.ANY))
        args.append(full)
        aliases = {2: 0}
    return pl.pallas_call(
        _negate_body,
        grid=(3,),
        in_specs=in_specs,
        out_specs=pl.BlockSpec((1, step, width), lambda i: (s, i, at // width)),
        out_shape=jax.ShapeDtypeStruct(shape, jnp.float32),
        input_output_aliases=aliases,
        compiler_params=pltpu.CompilerParams(vmem_limit_bytes=32 * 2**20),
        cost_estimate=pl.CostEstimate(
            flops=2 * nrows * width, bytes_accessed=12 * nrows * width, transcendentals=0
        ),
    )(*args)


def after(value, *deps):
    return lax.optimization_barrier((value, *deps))[0]


def grid_path(sigma_anc, factor_rows, diag_inverse, row_pattern, anc_pattern):
    ncol = lax.axis_size("col")
    r = lax.axis_index("row")
    c = lax.axis_index("col")
    z, x = c // 2, c % 2
    ns, own_rows, width = factor_rows.shape
    grid_rows, grid_cols = sigma_anc.shape

    mesh_pairs = lambda f, who: [(f(i), i) for i in range(ncol) if i // 2 in who]
    every, ends, mids = (0, 1, 2, 3), (0, 3), (1, 2)
    inner = lambda i: i + 2 if i < ncol // 2 else i - 2

    def recv(frm, v, who=every):
        return lax.ppermute(v, "col", mesh_pairs(frm, who))

    ox = lambda i: i ^ 1
    za = lambda i: i ^ 2
    zb = lambda i: i ^ 4

    row_mask = jnp.repeat(row_pattern.astype(jnp.float32), BLK, axis=1)
    local = lax.dynamic_slice_in_dim(row_mask, (r * ncol + c) * own_rows, own_rows, 1)
    lower = factor_rows * local[:, :, None]
    scale = lambda s, at, w: jnp.dot(lower[s], diag_inverse[s][:, at : at + w], precision=HIGH)

    mask = lax.dynamic_slice(
        anc_pattern,
        (c * (grid_rows // BLK), r * (grid_cols // BLK)),
        (grid_rows // BLK, grid_cols // BLK),
    ).reshape(-1)
    planes = (z, z ^ 1, jnp.where(z < 2, 2, 1), jnp.where(z < 2, 3, 0))
    near = [2 * p + x for p in planes]
    far = [2 * p + 1 - x for p in planes]

    def add(acc, *terms):
        return accumulate(acc, sigma_anc, mask, [i for i, _ in terms], [p for _, p in terms])

    def tdot(a, b, precision):
        dims = (((0,), (0,)), ((), ()))
        return lax.dot_general(a, b, dims, precision=precision)

    a0, b0 = lax.optimization_barrier((scale(0, 0, width), scale(1, 0, width)))
    a1, ax0, am = recv(za, a0), recv(ox, a0), recv(inner, a0, mids)
    b1, bx0 = recv(za, b0), recv(ox, b0)
    acc_a = add(None, (near[0], a0))
    acc_b = add(None, (near[0], b0))
    bm = recv(inner, after(b0, am), mids)
    square = jnp.concatenate([tdot(d, d, HIGHEST) for d in (diag_inverse[0], diag_inverse[1])])
    a1, ax0, am, b1, bx0, bm, acc_a, acc_b, square = lax.optimization_barrier(
        (a1, ax0, am, b1, bx0, bm, acc_a, acc_b, square)
    )
    ae, an, ax1 = recv(inner, am, ends), recv(inner, a1, mids), recv(ox, a1)
    be, bn = recv(inner, bm, ends), recv(inner, b1, mids)
    acc_a = add(acc_a, (far[0], ax0), (near[1], a1))
    acc_b = add(acc_b, (far[0], bx0), (near[1], b1))
    a2 = am + ae
    ax2 = recv(ox, after(a2, acc_a, acc_b))
    ax1, ax2, an, bn, a2, be, acc_a, acc_b = lax.optimization_barrier(
        (ax1, ax2, an, bn, a2, be, acc_a, acc_b)
    )
    b2 = bm + be
    af, bf, bx2 = recv(inner, an, ends), recv(inner, bn, ends), recv(ox, b2)
    acc_a = add(acc_a, (far[1], ax1), (near[2], a2))
    acc_b = add(acc_b, (near[2], b2))
    a3 = an + af
    ax3 = recv(ox, after(a3, acc_a, acc_b))
    acc_a = add(acc_a, (near[3], a3), (far[2], ax2))
    bf, bn, ax3, bx2, bx0, acc_a, acc_b = lax.optimization_barrier(
        (bf, bn, ax3, bx2, bx0, acc_a, acc_b)
    )
    b3 = bn + bf
    bx1, bx3 = recv(za, bx0), recv(ox, b3)
    acc_a = add(acc_a, (far[3], after(ax3, b3)))

    own_r = lambda i: i // (ncol // 2)
    holder = lambda i: own_r(i) * ncol + i
    other = lambda i: (1 - own_r(i)) * ncol + i
    is_holder = r == c // (ncol // 2)
    wanted = c % (ncol // 2)

    def recv_holder(frm, v):
        pairs = [(holder(frm(i)), holder(i)) for i in range(ncol)]
        return lax.ppermute(v, ("row", "col"), pairs)

    def choose(p0, p1, p2, p3):
        first = jnp.where(wanted == planes[0], p0, p1)
        second = jnp.where(wanted == planes[2], p2, p3)
        return jnp.where((wanted == planes[0]) | (wanted == planes[1]), first, second)

    def total(term, parts, work):
        size = term.shape[0] // parts // 8 * 8
        cuts = [i * size for i in range(parts)] + [term.shape[0]]
        ways = [ox, za, zb]
        values = [term[cuts[k] : cuts[k + 1]] for k in range(parts)]
        for step in range(3):
            values = [v + recv_holder(ways[(k + step) % 3], v) for k, v in enumerate(values)]
            if step < len(work):
                values = [after(v, work[step]) for v in values]
        return jnp.concatenate(values)

    def local_term(acc, got, same, cros):
        same, cros = choose(*same), choose(*cros)
        cross = -(acc + got)
        out_same = lax.dynamic_slice_in_dim(cross, x * own_rows, own_rows, 0)
        out_cros = lax.dynamic_slice_in_dim(cross, (1 - x) * own_rows, own_rows, 0)
        return tdot(same, out_same, HIGH) + tdot(cros, out_cros, HIGH)

    swap = lambda v: lax.ppermute(v, "row", [(0, 1), (1, 0)])
    shape = (ns, grid_rows, width)
    got_a = swap(acc_a)
    acc_b = add(acc_b, (near[3], after(b3, got_a)), (far[2], bx2))
    got_a = after(got_a, acc_b)
    term_a = local_term(acc_a, got_a, (a0, a1, a2, a3), (ax0, ax1, ax2, ax3))
    acc_b = add(acc_b, (far[1], bx1), (far[3], after(bx3, term_a)))
    got_b = swap(acc_b)
    term_b = local_term(acc_b, got_b, (b0, b1, b2, b3), (bx0, bx1, bx2, bx3))
    half = negate_into(None, acc_a, got_a, shape, 0, 0)
    full = negate_into(half, acc_b, got_b, shape, 1, 0)
    term = total(jnp.concatenate([term_a, term_b]), 3, (half, full))
    pairs = [(holder(i), other(i)) for i in range(ncol)]
    term = jnp.where(is_holder, term, lax.ppermute(term, ("row", "col"), pairs))
    return full, (square - term).reshape(diag_inverse.shape)


def plain_path(sigma_anc, factor_rows, diag_inverse, row_pattern, anc_pattern):
    nrow = lax.axis_size("row")
    ncol = lax.axis_size("col")
    r = lax.axis_index("row")
    c = lax.axis_index("col")
    own_rows = factor_rows.shape[1]
    grid_rows, grid_cols = sigma_anc.shape
    row_mask = jnp.repeat(row_pattern.astype(jnp.float32), BLK, axis=1)
    local = lax.dynamic_slice_in_dim(row_mask, (r * ncol + c) * own_rows, own_rows, 1)
    lower = factor_rows * local[:, :, None]
    scaled = jnp.einsum("sgb,sbc->sgc", lower, diag_inverse, precision=HIGHEST)
    piece = lax.all_gather(scaled, "col", axis=1, tiled=True)
    anc = jnp.repeat(anc_pattern.astype(jnp.float32), BLK, axis=0)
    anc = lax.dynamic_slice_in_dim(anc, c * grid_rows, grid_rows, 0)
    anc = jnp.repeat(anc, BLK, axis=1)
    anc = lax.dynamic_slice_in_dim(anc, r * grid_cols, grid_cols, 1)
    total = jnp.einsum("fg,sgc->sfc", sigma_anc * anc, piece, precision=HIGHEST)
    cross = -lax.psum(total, "row")
    half = c // (ncol // nrow)
    start = (c % (ncol // nrow)) * grid_rows
    mine = lax.dynamic_slice_in_dim(piece, start, grid_rows, 1)
    mine = jnp.where(r == half, mine, 0.0)
    term = jnp.einsum("sfc,sfd->scd", mine, cross, precision=HIGHEST)
    term = lax.psum(term, ("row", "col"))
    square = jnp.einsum("sbc,sbd->scd", diag_inverse, diag_inverse, precision=HIGHEST)
    return cross, square - term


def on_device(sigma_anc, factor_rows, diag_inverse, row_pattern, anc_pattern):
    own_rows, ncol = factor_rows.shape[1], lax.axis_size("col")
    fits = (
        ncol == 8
        and lax.axis_size("row") == 2
        and own_rows % BLK == 0
        and factor_rows.shape[0] == 2
        and sigma_anc.shape[0] % (3 * BLK) == 0
    )
    path = grid_path if fits else plain_path
    return path(sigma_anc, factor_rows, diag_inverse, row_pattern, anc_pattern)


def solution(mesh):
    in_specs = (
        P(("parts", "col"), "row"),
        P("parts", ("row", "col"), None),
        P("parts", None, None),
        P("parts", None),
        P("parts", None),
    )
    out_specs = (P("parts", "col", None), P("parts", None, None))
    return jax.shard_map(
        on_device, mesh=mesh, in_specs=in_specs, out_specs=out_specs, check_vma=False
    )
```

```python
import functools

import jax
import jax.numpy as jnp
from jax import lax
from jax.experimental import pallas as pl
from jax.experimental.pallas import tpu as pltpu
from jax.sharding import PartitionSpec as P

BLK = 128
HIGH = lax.Precision.HIGH
HIGHEST = lax.Precision.HIGHEST


def _accumulate_body(n, row_step, ncols_blk, has_acc, tab, mask, *refs):
    pieces, refs = refs[:n], refs[n:]
    a_ref = refs[0]
    acc_ref = refs[1] if has_acc else None
    out_ref, u_ref = refs[-2:]
    depth = pieces[0].shape[0]
    t = pl.program_id(0)

    @pl.when(t == 0)
    def _():
        if has_acc:
            out_ref[...] = acc_ref[...]
        else:
            out_ref[...] = jnp.zeros_like(out_ref)

    for k, piece in enumerate(pieces):

        @pl.when(t == k)
        def _(piece=piece):
            v = piece[...]
            hi = v.astype(jnp.bfloat16)
            u_ref[0:depth, :] = hi
            u_ref[depth : 2 * depth, :] = (v - hi.astype(jnp.float32)).astype(jnp.bfloat16)
            u_ref[2 * depth : 3 * depth, :] = hi

    per = depth // BLK
    col0 = tab[t] * per
    lane = lax.broadcasted_iota(jnp.int32, (1, depth), 1) // BLK
    for m in range(a_ref.shape[0] // row_step):
        rows = []
        for b in range(row_step // BLK):
            blk = m * (row_step // BLK) + b
            keep = jnp.zeros((1, depth), jnp.float32)
            for j in range(per):
                kept = mask[blk * ncols_blk + col0 + j].astype(jnp.float32)
                keep = jnp.where(lane == j, kept, keep)
            rows.append(a_ref[blk * BLK : (blk + 1) * BLK, :] * keep)
        a = jnp.concatenate(rows, axis=0)
        hi = a.astype(jnp.bfloat16)
        lo = (a - hi.astype(jnp.float32)).astype(jnp.bfloat16)
        lhs = jnp.concatenate([hi, hi, lo], axis=1)
        at = slice(m * row_step, (m + 1) * row_step)
        out_ref[at, :] += jnp.dot(lhs, u_ref[...], preferred_element_type=jnp.float32)


def accumulate(acc, sigma, mask, table, pieces, light=1):
    nrows, ncols = sigma.shape
    depth, width = pieces[0].shape
    n = len(pieces)
    row_step = next(s for s in (512, 256, 128) if nrows % s == 0)
    whole = lambda shape: pl.BlockSpec(shape, lambda t, *_: (0, 0), pipeline_mode=pl.Buffered(1))
    in_specs = [whole(p.shape) for p in pieces]
    in_specs.append(pl.BlockSpec((nrows, depth), lambda t, tab, mask: (0, tab[t])))
    args = [*pieces, sigma]
    if acc is not None:
        in_specs.append(whole(acc.shape))
        args.append(acc)
    return pl.pallas_call(
        functools.partial(_accumulate_body, n, row_step, ncols // BLK, acc is not None),
        grid_spec=pltpu.PrefetchScalarGridSpec(
            num_scalar_prefetch=2,
            grid=(n,),
            in_specs=in_specs,
            out_specs=whole((nrows, width)),
            scratch_shapes=[pltpu.VMEM((3 * depth, width), jnp.bfloat16)],
        ),
        out_shape=jax.ShapeDtypeStruct((nrows, width), jnp.float32),
        compiler_params=pltpu.CompilerParams(
            dimension_semantics=("arbitrary",), vmem_limit_bytes=48 * 2**20
        ),
        cost_estimate=pl.CostEstimate(
            flops=6 * n * depth * nrows * width // light,
            bytes_accessed=4 * n * depth * (nrows + width) // light,
            transcendentals=0,
        ),
    )(jnp.stack(table), mask, *args)


def _finish_body(count, place, *refs):
    pieces, refs = refs[: 2 * count], refs[2 * count :]
    acc_ref, got_ref = refs[:2]
    cross_ref, term_ref, rows_ref, sem = refs[-4:]
    t = pl.program_id(0)
    for half in range(2):
        for k in range(count):

            @pl.when((t == 0) & (place[1] == k))
            def _(half=half, k=k):
                piece = pieces[half * count + k]
                pltpu.make_async_copy(piece, rows_ref.at[half], sem.at[half]).start()

        @pl.when(t == half)
        def _(half=half):
            pltpu.make_async_copy(pieces[0], rows_ref.at[half], sem.at[half]).wait()

    halves = lambda v: (v.astype(jnp.bfloat16), v - v.astype(jnp.bfloat16).astype(jnp.float32))
    cross = -(acc_ref[...] + got_ref[...])
    cross_ref[0] = cross
    c_hi, c_lo = halves(cross)
    u_hi, u_lo = halves(rows_ref[t])
    c_lo, u_lo = c_lo.astype(jnp.bfloat16), u_lo.astype(jnp.bfloat16)

    def dot(u, v):
        dims = (((0,), (0,)), ((), ()))
        return lax.dot_general(u, v, dims, preferred_element_type=jnp.float32)

    term = dot(u_hi, c_hi) + (dot(u_hi, c_lo) + dot(u_lo, c_hi))

    @pl.when(t == 0)
    def _():
        term_ref[...] = term

    @pl.when(t > 0)
    def _():
        term_ref[...] += term


def finish(full, acc, got, place, near, far, shape, s):
    depth, width = near[0].shape
    anywhere = pl.BlockSpec(memory_space=pl.ANY)
    tile = pl.BlockSpec((depth, width), lambda t, place: ((t + place[0]) % 2, 0))
    args = [*near, *far, acc, got]
    in_specs = [anywhere] * (len(near) + len(far)) + [tile, tile]
    aliases = {}
    if full is not None:
        aliases = {len(args) + 1: 0}
        args.append(full)
        in_specs.append(anywhere)
    return pl.pallas_call(
        functools.partial(_finish_body, len(near)),
        grid_spec=pltpu.PrefetchScalarGridSpec(
            num_scalar_prefetch=1,
            grid=(2,),
            in_specs=in_specs,
            out_specs=[
                pl.BlockSpec((1, depth, width), lambda t, place: (s, (t + place[0]) % 2, 0)),
                pl.BlockSpec((width, width), lambda t, place: (0, 0)),
            ],
            scratch_shapes=[
                pltpu.VMEM((2, depth, width), jnp.float32),
                pltpu.SemaphoreType.DMA((2,)),
            ],
        ),
        out_shape=[
            jax.ShapeDtypeStruct(shape, jnp.float32),
            jax.ShapeDtypeStruct((width, width), jnp.float32),
        ],
        input_output_aliases=aliases,
        compiler_params=pltpu.CompilerParams(
            dimension_semantics=("arbitrary",), vmem_limit_bytes=40 * 2**20
        ),
        cost_estimate=pl.CostEstimate(
            flops=depth * width, bytes_accessed=depth * width, transcendentals=0
        ),
    )(place, *args)


def after(value, *deps):
    return lax.optimization_barrier((value, *deps))[0]


def grid_path(sigma_anc, factor_rows, diag_inverse, row_pattern, anc_pattern):
    ncol = lax.axis_size("col")
    r = lax.axis_index("row")
    c = lax.axis_index("col")
    z, x = c // 2, c % 2
    ns, own_rows, width = factor_rows.shape
    grid_rows, grid_cols = sigma_anc.shape

    mesh_pairs = lambda f, who: [(f(i), i) for i in range(ncol) if i // 2 in who]
    every, ends, mids = (0, 1, 2, 3), (0, 3), (1, 2)
    inner = lambda i: i + 2 if i < ncol // 2 else i - 2

    def recv(frm, v, who=every):
        return lax.ppermute(v, "col", mesh_pairs(frm, who))

    ox = lambda i: i ^ 1
    za = lambda i: i ^ 2
    outer = lambda i: i - 2 if i < ncol // 2 else i + 2

    row_mask = jnp.repeat(row_pattern.astype(jnp.float32), BLK, axis=1)
    local = lax.dynamic_slice_in_dim(row_mask, (r * ncol + c) * own_rows, own_rows, 1)
    lower = factor_rows * local[:, :, None]
    scale = lambda s, at, w: jnp.dot(lower[s], diag_inverse[s][:, at : at + w], precision=HIGH)

    mask = lax.dynamic_slice(
        anc_pattern,
        (c * (grid_rows // BLK), r * (grid_cols // BLK)),
        (grid_rows // BLK, grid_cols // BLK),
    ).reshape(-1)
    planes = (z, z ^ 1, jnp.where(z < 2, 2, 1), jnp.where(z < 2, 3, 0))
    near = [2 * p + x for p in planes]
    far = [2 * p + 1 - x for p in planes]

    def add(acc, *terms, light=1):
        tables, pieces = [i for i, _ in terms], [p for _, p in terms]
        return accumulate(acc, sigma_anc, mask, tables, pieces, light)

    def tdot(a, b, precision):
        dims = (((0,), (0,)), ((), ()))
        return lax.dot_general(a, b, dims, precision=precision)

    a0, b0 = lax.optimization_barrier((scale(0, 0, width), scale(1, 0, width)))
    ax0, a1, am = recv(ox, a0), recv(za, a0), recv(inner, a0, mids)
    b1, bx0 = recv(za, b0), recv(ox, b0)
    acc_a = add(None, (near[0], a0))
    acc_b = add(None, (near[0], b0))
    bm = recv(inner, after(b0, am), mids)
    square = jnp.stack([tdot(diag_inverse[i], diag_inverse[i], HIGHEST) for i in range(ns)])
    a1, ax0, am, acc_a, acc_b, square = lax.optimization_barrier(
        (a1, ax0, am, acc_a, acc_b, square)
    )
    ae, an, ax1 = recv(inner, am, ends), recv(inner, a1, mids), recv(ox, a1)
    be, bn = recv(inner, bm, ends), recv(inner, b1, mids)
    acc_a = add(acc_a, (far[0], ax0), (near[1], a1))
    acc_b = add(acc_b, (far[0], bx0), (near[1], b1))
    a2 = am + ae
    ax2 = recv(ox, after(a2, acc_a, acc_b))
    ax1, an, bn, a2, bm, be, acc_a, acc_b = lax.optimization_barrier(
        (ax1, an, bn, a2, bm, be, acc_a, acc_b)
    )
    b2 = bm + be
    af, bf, bx2 = recv(inner, an, ends), recv(inner, bn, ends), recv(ox, b2)
    acc_b = add(acc_b, (near[2], after(b2, ax2)))
    acc_a = add(acc_a, (far[1], after(ax1, ax2)), (near[2], a2))
    a3 = an + af
    ax3 = recv(ox, after(a3, acc_a, acc_b))
    acc_a = add(acc_a, (near[3], a3), (far[2], ax2))
    bf, bn, bx0, acc_a, acc_b = lax.optimization_barrier((bf, bn, bx0, acc_a, acc_b))
    b3 = bn + bf
    bx1, bx3 = recv(za, bx0), recv(ox, b3)
    acc_b = add(acc_b, (near[3], b3), (far[2], bx2), light=1000)
    acc_a = add(acc_a, (far[3], after(ax3, acc_b)), light=1000)

    own_r = lambda i: i // (ncol // 2)
    holder = lambda i: own_r(i) * ncol + i
    other = lambda i: (1 - own_r(i)) * ncol + i
    is_holder = r == c // (ncol // 2)
    def recv_holder(frm, v, who=every):
        pairs = [(holder(src), holder(dst)) for src, dst in mesh_pairs(frm, who)]
        return lax.ppermute(v, ("row", "col"), pairs)

    def total(term):
        size = term.shape[0] // 2
        low, high = term[:size], term[size:]
        v = jnp.where(x == 0, low, high) + recv_holder(ox, jnp.where(x == 0, high, low))
        v = v + recv_holder(outer, v, mids)
        v = v + recv_holder(inner, v, mids)
        v = jnp.where((z == 0) | (z == 3), recv_holder(inner, v, ends), v)
        w = recv_holder(ox, v)
        term = jnp.where(x == 0, jnp.concatenate([v, w]), jnp.concatenate([w, v]))
        pairs = [(holder(i), other(i)) for i in range(ncol)]
        return jnp.where(is_holder, term, lax.ppermute(term, ("row", "col"), pairs))

    wanted = c % (ncol // 2)
    pick = sum(k * (wanted == p).astype(jnp.int32) for k, p in enumerate(planes))
    place = jnp.stack([x, pick])
    swap = lambda v: lax.ppermute(v, "row", [(0, 1), (1, 0)])
    shape = (ns, grid_rows, width)
    got_a = swap(acc_a)
    acc_b = add(acc_b, (far[1], bx1), (far[3], bx3))
    got_b = swap(acc_b)
    got_a = after(got_a, acc_b)
    full, term_a = finish(None, acc_a, got_a, place, (a0, a1, a2, a3), (ax0, ax1, ax2, ax3), shape, 0)
    full, term_b = finish(full, acc_b, got_b, place, (b0, b1, b2, b3), (bx0, bx1, bx2, bx3), shape, 1)
    return full, square - jnp.stack([total(term_a), total(term_b)])


def plain_path(sigma_anc, factor_rows, diag_inverse, row_pattern, anc_pattern):
    nrow = lax.axis_size("row")
    ncol = lax.axis_size("col")
    r = lax.axis_index("row")
    c = lax.axis_index("col")
    own_rows = factor_rows.shape[1]
    grid_rows, grid_cols = sigma_anc.shape
    row_mask = jnp.repeat(row_pattern.astype(jnp.float32), BLK, axis=1)
    local = lax.dynamic_slice_in_dim(row_mask, (r * ncol + c) * own_rows, own_rows, 1)
    lower = factor_rows * local[:, :, None]
    scaled = jnp.einsum("sgb,sbc->sgc", lower, diag_inverse, precision=HIGHEST)
    piece = lax.all_gather(scaled, "col", axis=1, tiled=True)
    anc = jnp.repeat(anc_pattern.astype(jnp.float32), BLK, axis=0)
    anc = lax.dynamic_slice_in_dim(anc, c * grid_rows, grid_rows, 0)
    anc = jnp.repeat(anc, BLK, axis=1)
    anc = lax.dynamic_slice_in_dim(anc, r * grid_cols, grid_cols, 1)
    total = jnp.einsum("fg,sgc->sfc", sigma_anc * anc, piece, precision=HIGHEST)
    cross = -lax.psum(total, "row")
    half = c // (ncol // nrow)
    start = (c % (ncol // nrow)) * grid_rows
    mine = lax.dynamic_slice_in_dim(piece, start, grid_rows, 1)
    mine = jnp.where(r == half, mine, 0.0)
    term = jnp.einsum("sfc,sfd->scd", mine, cross, precision=HIGHEST)
    term = lax.psum(term, ("row", "col"))
    square = jnp.einsum("sbc,sbd->scd", diag_inverse, diag_inverse, precision=HIGHEST)
    return cross, square - term


def on_device(sigma_anc, factor_rows, diag_inverse, row_pattern, anc_pattern):
    own_rows, ncol = factor_rows.shape[1], lax.axis_size("col")
    fits = (
        ncol == 8
        and lax.axis_size("row") == 2
        and own_rows % BLK == 0
        and factor_rows.shape[0] == 2
        and sigma_anc.shape[0] % (3 * BLK) == 0
    )
    path = grid_path if fits else plain_path
    return path(sigma_anc, factor_rows, diag_inverse, row_pattern, anc_pattern)


def solution(mesh):
    in_specs = (
        P(("parts", "col"), "row"),
        P("parts", ("row", "col"), None),
        P("parts", None, None),
        P("parts", None),
        P("parts", None),
    )
    out_specs = (P("parts", "col", None), P("parts", None, None))
    return jax.shard_map(
        on_device, mesh=mesh, in_specs=in_specs, out_specs=out_specs, check_vma=False
    )
```

```python
import functools

import jax
import jax.numpy as jnp
from jax import lax
from jax.experimental import pallas as pl
from jax.experimental.pallas import tpu as pltpu
from jax.sharding import PartitionSpec as P

BLK = 128
HIGH = lax.Precision.HIGH
HIGHEST = lax.Precision.HIGHEST


def _accumulate_body(n, ncols_blk, has_acc, tab, mask, *refs):
    pieces, tiles, refs = refs[:n], refs[n : 2 * n], refs[2 * n :]
    acc_ref = refs[0] if has_acc else None
    out_ref, u_ref = refs[-2:]
    depth = pieces[0].shape[0]
    rows = out_ref.shape[0]
    m = pl.program_id(0)

    @pl.when(m == 0)
    def _():
        for k, piece in enumerate(pieces):
            v, at = piece[...], 3 * k * depth
            hi = v.astype(jnp.bfloat16)
            u_ref[at : at + depth, :] = hi
            u_ref[at + depth : at + 2 * depth, :] = (v - hi.astype(jnp.float32)).astype(
                jnp.bfloat16
            )
            u_ref[at + 2 * depth : at + 3 * depth, :] = hi

    per = depth // BLK
    lane = lax.broadcasted_iota(jnp.int32, (1, depth), 1) // BLK
    lhs = []
    for k, tile in enumerate(tiles):
        col0 = tab[k] * per
        kept = []
        for b in range(rows // BLK):
            row0 = (m * (rows // BLK) + b) * ncols_blk + col0
            keep = jnp.zeros((1, depth), jnp.float32)
            for j in range(per):
                keep = jnp.where(lane == j, mask[row0 + j].astype(jnp.float32), keep)
            kept.append(tile[b * BLK : (b + 1) * BLK, :] * keep)
        a = jnp.concatenate(kept, axis=0)
        hi = a.astype(jnp.bfloat16)
        lo = (a - hi.astype(jnp.float32)).astype(jnp.bfloat16)
        lhs += [hi, hi, lo]
    total = jnp.dot(
        jnp.concatenate(lhs, axis=1), u_ref[...], preferred_element_type=jnp.float32
    )
    out_ref[...] = total + acc_ref[...] if has_acc else total


def accumulate(acc, sigma, mask, table, pieces, light=1):
    nrows, ncols = sigma.shape
    depth, width = pieces[0].shape
    n = len(pieces)
    step = next(s for s in (256, 128) if nrows % s == 0)
    whole = lambda shape: pl.BlockSpec(shape, lambda m, *_: (0, 0), pipeline_mode=pl.Buffered(1))
    rows = pl.BlockSpec((step, width), lambda m, *_: (m, 0))
    tile = lambda k: pl.BlockSpec((step, depth), lambda m, tab, mask: (m, tab[k]))
    in_specs = [whole(p.shape) for p in pieces] + [tile(k) for k in range(n)]
    args = [*pieces, *[sigma] * n]
    if acc is not None:
        in_specs.append(rows)
        args.append(acc)
    return pl.pallas_call(
        functools.partial(_accumulate_body, n, ncols // BLK, acc is not None),
        grid_spec=pltpu.PrefetchScalarGridSpec(
            num_scalar_prefetch=2,
            grid=(nrows // step,),
            in_specs=in_specs,
            out_specs=rows,
            scratch_shapes=[pltpu.VMEM((3 * n * depth, width), jnp.bfloat16)],
        ),
        out_shape=jax.ShapeDtypeStruct((nrows, width), jnp.float32),
        compiler_params=pltpu.CompilerParams(
            dimension_semantics=("arbitrary",), vmem_limit_bytes=48 * 2**20
        ),
        cost_estimate=pl.CostEstimate(
            flops=6 * n * depth * nrows * width // light,
            bytes_accessed=4 * n * depth * (nrows + width) // light,
            transcendentals=0,
        ),
    )(jnp.stack(table), mask, *args)


def _finish_body(count, place, *refs):
    pieces, refs = refs[: 2 * count], refs[2 * count :]
    acc_ref, got_ref = refs[:2]
    cross_ref, term_ref, rows_ref, sem = refs[-4:]
    t = pl.program_id(0)
    for half in range(2):
        for k in range(count):

            @pl.when((t == 0) & (place[1] == k))
            def _(half=half, k=k):
                piece = pieces[half * count + k]
                pltpu.make_async_copy(piece, rows_ref.at[half], sem.at[half]).start()

        @pl.when(t == half)
        def _(half=half):
            pltpu.make_async_copy(pieces[0], rows_ref.at[half], sem.at[half]).wait()

    halves = lambda v: (v.astype(jnp.bfloat16), v - v.astype(jnp.bfloat16).astype(jnp.float32))
    cross = -(acc_ref[...] + got_ref[...])
    cross_ref[0] = cross
    c_hi, c_lo = halves(cross)
    u_hi, u_lo = halves(rows_ref[t])
    c_lo, u_lo = c_lo.astype(jnp.bfloat16), u_lo.astype(jnp.bfloat16)

    def dot(u, v):
        dims = (((0,), (0,)), ((), ()))
        return lax.dot_general(u, v, dims, preferred_element_type=jnp.float32)

    term = dot(u_hi, c_hi) + (dot(u_hi, c_lo) + dot(u_lo, c_hi))

    @pl.when(t == 0)
    def _():
        term_ref[...] = term

    @pl.when(t > 0)
    def _():
        term_ref[...] += term


def finish(full, acc, got, place, near, far, shape, s):
    depth, width = near[0].shape
    anywhere = pl.BlockSpec(memory_space=pl.ANY)
    tile = pl.BlockSpec((depth, width), lambda t, place: ((t + place[0]) % 2, 0))
    args = [*near, *far, acc, got]
    in_specs = [anywhere] * (len(near) + len(far)) + [tile, tile]
    aliases = {}
    if full is not None:
        aliases = {len(args) + 1: 0}
        args.append(full)
        in_specs.append(anywhere)
    return pl.pallas_call(
        functools.partial(_finish_body, len(near)),
        grid_spec=pltpu.PrefetchScalarGridSpec(
            num_scalar_prefetch=1,
            grid=(2,),
            in_specs=in_specs,
            out_specs=[
                pl.BlockSpec((1, depth, width), lambda t, place: (s, (t + place[0]) % 2, 0)),
                pl.BlockSpec((width, width), lambda t, place: (0, 0)),
            ],
            scratch_shapes=[
                pltpu.VMEM((2, depth, width), jnp.float32),
                pltpu.SemaphoreType.DMA((2,)),
            ],
        ),
        out_shape=[
            jax.ShapeDtypeStruct(shape, jnp.float32),
            jax.ShapeDtypeStruct((width, width), jnp.float32),
        ],
        input_output_aliases=aliases,
        compiler_params=pltpu.CompilerParams(
            dimension_semantics=("arbitrary",), vmem_limit_bytes=40 * 2**20
        ),
        cost_estimate=pl.CostEstimate(
            flops=depth * width, bytes_accessed=depth * width, transcendentals=0
        ),
    )(place, *args)


def after(value, *deps):
    return lax.optimization_barrier((value, *deps))[0]


def grid_path(sigma_anc, factor_rows, diag_inverse, row_pattern, anc_pattern):
    ncol = lax.axis_size("col")
    r = lax.axis_index("row")
    c = lax.axis_index("col")
    z, x = c // 2, c % 2
    ns, own_rows, width = factor_rows.shape
    grid_rows, grid_cols = sigma_anc.shape

    mesh_pairs = lambda f, who: [(f(i), i) for i in range(ncol) if i // 2 in who]
    every, ends, mids = (0, 1, 2, 3), (0, 3), (1, 2)
    inner = lambda i: i + 2 if i < ncol // 2 else i - 2

    def recv(frm, v, who=every):
        return lax.ppermute(v, "col", mesh_pairs(frm, who))

    ox = lambda i: i ^ 1
    za = lambda i: i ^ 2
    outer = lambda i: i - 2 if i < ncol // 2 else i + 2

    row_mask = jnp.repeat(row_pattern.astype(jnp.float32), BLK, axis=1)
    local = lax.dynamic_slice_in_dim(row_mask, (r * ncol + c) * own_rows, own_rows, 1)
    lower = factor_rows * local[:, :, None]
    scale = lambda s, at, w: jnp.dot(lower[s], diag_inverse[s][:, at : at + w], precision=HIGH)

    mask = lax.dynamic_slice(
        anc_pattern,
        (c * (grid_rows // BLK), r * (grid_cols // BLK)),
        (grid_rows // BLK, grid_cols // BLK),
    ).reshape(-1)
    planes = (z, z ^ 1, jnp.where(z < 2, 2, 1), jnp.where(z < 2, 3, 0))
    near = [2 * p + x for p in planes]
    far = [2 * p + 1 - x for p in planes]

    def add(acc, *terms, light=1):
        tables, pieces = [i for i, _ in terms], [p for _, p in terms]
        return accumulate(acc, sigma_anc, mask, tables, pieces, light)

    def tdot(a, b, precision):
        dims = (((0,), (0,)), ((), ()))
        return lax.dot_general(a, b, dims, precision=precision)

    own_r = lambda i: i // (ncol // 2)
    holder = lambda i: own_r(i) * ncol + i
    other = lambda i: (1 - own_r(i)) * ncol + i
    is_holder = r == c // (ncol // 2)

    def recv_holder(frm, v, who=every):
        pairs = [(holder(src), holder(dst)) for src, dst in mesh_pairs(frm, who)]
        return lax.ppermute(v, ("row", "col"), pairs)

    def total(term):
        size = term.shape[0] // 2
        low, high = term[:size], term[size:]
        v = jnp.where(x == 0, low, high) + recv_holder(ox, jnp.where(x == 0, high, low))
        v = v + recv_holder(outer, v, mids)
        v = v + recv_holder(inner, v, mids)
        v = jnp.where((z == 0) | (z == 3), recv_holder(inner, v, ends), v)
        w = recv_holder(ox, v)
        term = jnp.where(x == 0, jnp.concatenate([v, w]), jnp.concatenate([w, v]))
        pairs = [(holder(i), other(i)) for i in range(ncol)]
        return jnp.where(is_holder, term, lax.ppermute(term, ("row", "col"), pairs))

    wanted = c % (ncol // 2)
    pick = sum(k * (wanted == p).astype(jnp.int32) for k, p in enumerate(planes))
    place = jnp.stack([x, pick])
    swap = lambda v: lax.ppermute(v, "row", [(0, 1), (1, 0)])
    shape = (ns, grid_rows, width)

    a0, b0 = lax.optimization_barrier((scale(0, 0, width), scale(1, 0, width)))
    ax0, a1, am = recv(ox, a0), recv(za, a0), recv(inner, a0, mids)
    b1, bx0 = recv(za, b0), recv(ox, b0)
    acc_a = add(None, (near[0], a0))
    acc_b = add(None, (near[0], b0))
    bm = recv(inner, after(b0, am), mids)
    square = jnp.stack([tdot(diag_inverse[i], diag_inverse[i], HIGHEST) for i in range(ns)])
    a1, ax0, am, acc_a, acc_b, square = lax.optimization_barrier(
        (a1, ax0, am, acc_a, acc_b, square)
    )
    ae, an, ax1 = recv(inner, am, ends), recv(inner, a1, mids), recv(ox, a1)
    bn = recv(inner, b1, mids)
    af = recv(inner, an, ends)
    acc_a = add(acc_a, (far[0], ax0), (near[1], a1))
    acc_b = add(acc_b, (far[0], bx0), (near[1], b1))
    a2 = am + ae
    ax2 = recv(ox, after(a2, acc_a, acc_b))
    ax1, an, af, bn, a2, bm, acc_a, acc_b = lax.optimization_barrier(
        (ax1, an, af, bn, a2, bm, acc_a, acc_b)
    )
    a3 = an + af
    ax3 = recv(ox, a3)
    be, bf = recv(inner, bm, ends), recv(inner, bn, ends)
    acc_a = add(
        acc_a, (far[1], after(ax1, ax2)), (near[2], a2), (near[3], a3), (far[2], ax2), light=1000
    )
    b2 = after(bm + be, acc_a)
    bx2 = recv(ox, b2)
    acc_a = add(acc_a, (far[3], after(ax3, b2)), light=1000)
    got_a = swap(acc_a)
    bf, bn, bx0, bx2, acc_a = lax.optimization_barrier((bf, bn, bx0, bx2, acc_a))
    b3 = bn + bf
    bx1, bx3 = recv(za, bx0), recv(ox, b3)
    acc_b = add(acc_b, (near[2], b2), (near[3], b3), (far[2], bx2), light=1000)
    got_a = after(got_a, acc_b)
    full, term_a = finish(None, acc_a, got_a, place, (a0, a1, a2, a3), (ax0, ax1, ax2, ax3), shape, 0)
    acc_b = add(acc_b, (far[1], bx1), (far[3], after(bx3, term_a)))
    sum_a = total(term_a)
    got_b = swap(acc_b)
    full, term_b = finish(full, acc_b, got_b, place, (b0, b1, b2, b3), (bx0, bx1, bx2, bx3), shape, 1)
    return full, square - jnp.stack([sum_a, total(term_b)])


def plain_path(sigma_anc, factor_rows, diag_inverse, row_pattern, anc_pattern):
    nrow = lax.axis_size("row")
    ncol = lax.axis_size("col")
    r = lax.axis_index("row")
    c = lax.axis_index("col")
    own_rows = factor_rows.shape[1]
    grid_rows, grid_cols = sigma_anc.shape
    row_mask = jnp.repeat(row_pattern.astype(jnp.float32), BLK, axis=1)
    local = lax.dynamic_slice_in_dim(row_mask, (r * ncol + c) * own_rows, own_rows, 1)
    lower = factor_rows * local[:, :, None]
    scaled = jnp.einsum("sgb,sbc->sgc", lower, diag_inverse, precision=HIGHEST)
    piece = lax.all_gather(scaled, "col", axis=1, tiled=True)
    anc = jnp.repeat(anc_pattern.astype(jnp.float32), BLK, axis=0)
    anc = lax.dynamic_slice_in_dim(anc, c * grid_rows, grid_rows, 0)
    anc = jnp.repeat(anc, BLK, axis=1)
    anc = lax.dynamic_slice_in_dim(anc, r * grid_cols, grid_cols, 1)
    total = jnp.einsum("fg,sgc->sfc", sigma_anc * anc, piece, precision=HIGHEST)
    cross = -lax.psum(total, "row")
    half = c // (ncol // nrow)
    start = (c % (ncol // nrow)) * grid_rows
    mine = lax.dynamic_slice_in_dim(piece, start, grid_rows, 1)
    mine = jnp.where(r == half, mine, 0.0)
    term = jnp.einsum("sfc,sfd->scd", mine, cross, precision=HIGHEST)
    term = lax.psum(term, ("row", "col"))
    square = jnp.einsum("sbc,sbd->scd", diag_inverse, diag_inverse, precision=HIGHEST)
    return cross, square - term


def on_device(sigma_anc, factor_rows, diag_inverse, row_pattern, anc_pattern):
    own_rows, ncol = factor_rows.shape[1], lax.axis_size("col")
    fits = (
        ncol == 8
        and lax.axis_size("row") == 2
        and own_rows % BLK == 0
        and factor_rows.shape[0] == 2
        and sigma_anc.shape[0] % (3 * BLK) == 0
    )
    path = grid_path if fits else plain_path
    return path(sigma_anc, factor_rows, diag_inverse, row_pattern, anc_pattern)


def solution(mesh):
    in_specs = (
        P(("parts", "col"), "row"),
        P("parts", ("row", "col"), None),
        P("parts", None, None),
        P("parts", None),
        P("parts", None),
    )
    out_specs = (P("parts", "col", None), P("parts", None, None))
    return jax.shard_map(
        on_device, mesh=mesh, in_specs=in_specs, out_specs=out_specs, check_vma=False
    )
```

```python
import functools

import jax
import jax.numpy as jnp
from jax import lax
from jax.experimental import pallas as pl
from jax.experimental.pallas import tpu as pltpu
from jax.sharding import PartitionSpec as P

BLK = 128
HIGH = lax.Precision.HIGH
HIGHEST = lax.Precision.HIGHEST


def _accumulate_body(n, ncols_blk, has_acc, tab, mask, *refs):
    pieces, tiles, refs = refs[:n], refs[n : 2 * n], refs[2 * n :]
    acc_ref = refs[0] if has_acc else None
    out_ref, u_ref = refs[-2:]
    depth = pieces[0].shape[0]
    rows = out_ref.shape[0]
    m = pl.program_id(0)

    @pl.when(m == 0)
    def _():
        for k, piece in enumerate(pieces):
            v, at = piece[...], 3 * k * depth
            hi = v.astype(jnp.bfloat16)
            u_ref[at : at + depth, :] = hi
            u_ref[at + depth : at + 2 * depth, :] = (v - hi.astype(jnp.float32)).astype(
                jnp.bfloat16
            )
            u_ref[at + 2 * depth : at + 3 * depth, :] = hi

    per = depth // BLK
    lane = lax.broadcasted_iota(jnp.int32, (1, depth), 1) // BLK
    lhs = []
    for k, tile in enumerate(tiles):
        col0 = tab[k] * per
        kept = []
        for b in range(rows // BLK):
            row0 = (m * (rows // BLK) + b) * ncols_blk + col0
            keep = jnp.zeros((1, depth), jnp.float32)
            for j in range(per):
                keep = jnp.where(lane == j, mask[row0 + j].astype(jnp.float32), keep)
            kept.append(tile[b * BLK : (b + 1) * BLK, :] * keep)
        a = jnp.concatenate(kept, axis=0)
        hi = a.astype(jnp.bfloat16)
        lo = (a - hi.astype(jnp.float32)).astype(jnp.bfloat16)
        lhs += [hi, hi, lo]
    total = jnp.dot(
        jnp.concatenate(lhs, axis=1), u_ref[...], preferred_element_type=jnp.float32
    )
    out_ref[...] = total + acc_ref[...] if has_acc else total


def accumulate(acc, sigma, mask, table, pieces, light=1):
    nrows, ncols = sigma.shape
    depth, width = pieces[0].shape
    n = len(pieces)
    step = next(s for s in (512, 256, 128) if nrows % s == 0)
    whole = lambda shape: pl.BlockSpec(shape, lambda m, *_: (0, 0), pipeline_mode=pl.Buffered(1))
    rows = pl.BlockSpec((step, width), lambda m, *_: (m, 0))
    tile = lambda k: pl.BlockSpec((step, depth), lambda m, tab, mask: (m, tab[k]))
    in_specs = [whole(p.shape) for p in pieces] + [tile(k) for k in range(n)]
    args = [*pieces, *[sigma] * n]
    if acc is not None:
        in_specs.append(rows)
        args.append(acc)
    return pl.pallas_call(
        functools.partial(_accumulate_body, n, ncols // BLK, acc is not None),
        grid_spec=pltpu.PrefetchScalarGridSpec(
            num_scalar_prefetch=2,
            grid=(nrows // step,),
            in_specs=in_specs,
            out_specs=rows,
            scratch_shapes=[pltpu.VMEM((3 * n * depth, width), jnp.bfloat16)],
        ),
        out_shape=jax.ShapeDtypeStruct((nrows, width), jnp.float32),
        compiler_params=pltpu.CompilerParams(
            dimension_semantics=("arbitrary",), vmem_limit_bytes=48 * 2**20
        ),
        cost_estimate=pl.CostEstimate(
            flops=6 * n * depth * nrows * width // light,
            bytes_accessed=4 * n * depth * (nrows + width) // light,
            transcendentals=0,
        ),
    )(jnp.stack(table), mask, *args)


def _finish_body(count, place, *refs):
    pieces, refs = refs[: 2 * count], refs[2 * count :]
    acc_ref, got_ref = refs[:2]
    cross_ref, term_ref, rows_ref, sem = refs[-4:]
    t = pl.program_id(0)
    for half in range(2):
        for k in range(count):

            @pl.when((t == 0) & (place[1] == k))
            def _(half=half, k=k):
                piece = pieces[half * count + k]
                pltpu.make_async_copy(piece, rows_ref.at[half], sem.at[half]).start()

        @pl.when(t == half)
        def _(half=half):
            pltpu.make_async_copy(pieces[0], rows_ref.at[half], sem.at[half]).wait()

    halves = lambda v: (v.astype(jnp.bfloat16), v - v.astype(jnp.bfloat16).astype(jnp.float32))
    cross = -(acc_ref[...] + got_ref[...])
    cross_ref[0] = cross
    c_hi, c_lo = halves(cross)
    u_hi, u_lo = halves(rows_ref[t])
    c_lo, u_lo = c_lo.astype(jnp.bfloat16), u_lo.astype(jnp.bfloat16)

    def dot(u, v):
        dims = (((0,), (0,)), ((), ()))
        return lax.dot_general(u, v, dims, preferred_element_type=jnp.float32)

    term = dot(u_hi, c_hi) + (dot(u_hi, c_lo) + dot(u_lo, c_hi))

    @pl.when(t == 0)
    def _():
        term_ref[...] = term

    @pl.when(t > 0)
    def _():
        term_ref[...] += term


def finish(full, acc, got, place, near, far, shape, s):
    depth, width = near[0].shape
    anywhere = pl.BlockSpec(memory_space=pl.ANY)
    tile = pl.BlockSpec((depth, width), lambda t, place: ((t + place[0]) % 2, 0))
    args = [*near, *far, acc, got]
    in_specs = [anywhere] * (len(near) + len(far)) + [tile, tile]
    aliases = {}
    if full is not None:
        aliases = {len(args) + 1: 0}
        args.append(full)
        in_specs.append(anywhere)
    return pl.pallas_call(
        functools.partial(_finish_body, len(near)),
        grid_spec=pltpu.PrefetchScalarGridSpec(
            num_scalar_prefetch=1,
            grid=(2,),
            in_specs=in_specs,
            out_specs=[
                pl.BlockSpec((1, depth, width), lambda t, place: (s, (t + place[0]) % 2, 0)),
                pl.BlockSpec((width, width), lambda t, place: (0, 0)),
            ],
            scratch_shapes=[
                pltpu.VMEM((2, depth, width), jnp.float32),
                pltpu.SemaphoreType.DMA((2,)),
            ],
        ),
        out_shape=[
            jax.ShapeDtypeStruct(shape, jnp.float32),
            jax.ShapeDtypeStruct((width, width), jnp.float32),
        ],
        input_output_aliases=aliases,
        compiler_params=pltpu.CompilerParams(
            dimension_semantics=("arbitrary",), vmem_limit_bytes=40 * 2**20
        ),
        cost_estimate=pl.CostEstimate(
            flops=depth * width, bytes_accessed=depth * width, transcendentals=0
        ),
    )(place, *args)


def after(value, *deps):
    return lax.optimization_barrier((value, *deps))[0]


def grid_path(sigma_anc, factor_rows, diag_inverse, row_pattern, anc_pattern):
    ncol = lax.axis_size("col")
    r = lax.axis_index("row")
    c = lax.axis_index("col")
    z, x = c // 2, c % 2
    ns, own_rows, width = factor_rows.shape
    grid_rows, grid_cols = sigma_anc.shape

    mesh_pairs = lambda f, who: [(f(i), i) for i in range(ncol) if i // 2 in who]
    every, ends, mids = (0, 1, 2, 3), (0, 3), (1, 2)
    inner = lambda i: i + 2 if i < ncol // 2 else i - 2

    def recv(frm, v, who=every):
        return lax.ppermute(v, "col", mesh_pairs(frm, who))

    ox = lambda i: i ^ 1
    za = lambda i: i ^ 2
    outer = lambda i: i - 2 if i < ncol // 2 else i + 2

    row_mask = jnp.repeat(row_pattern.astype(jnp.float32), BLK, axis=1)
    local = lax.dynamic_slice_in_dim(row_mask, (r * ncol + c) * own_rows, own_rows, 1)
    lower = factor_rows * local[:, :, None]
    scale = lambda s, at, w: jnp.dot(lower[s], diag_inverse[s][:, at : at + w], precision=HIGH)

    mask = lax.dynamic_slice(
        anc_pattern,
        (c * (grid_rows // BLK), r * (grid_cols // BLK)),
        (grid_rows // BLK, grid_cols // BLK),
    ).reshape(-1)
    planes = (z, z ^ 1, jnp.where(z < 2, 2, 1), jnp.where(z < 2, 3, 0))
    near = [2 * p + x for p in planes]
    far = [2 * p + 1 - x for p in planes]

    def add(acc, *terms, light=1):
        tables, pieces = [i for i, _ in terms], [p for _, p in terms]
        return accumulate(acc, sigma_anc, mask, tables, pieces, light)

    def tdot(a, b, precision):
        dims = (((0,), (0,)), ((), ()))
        return lax.dot_general(a, b, dims, precision=precision)

    own_r = lambda i: i // (ncol // 2)
    holder = lambda i: own_r(i) * ncol + i
    other = lambda i: (1 - own_r(i)) * ncol + i
    is_holder = r == c // (ncol // 2)

    def recv_holder(frm, v, who=every):
        pairs = [(holder(src), holder(dst)) for src, dst in mesh_pairs(frm, who)]
        return lax.ppermute(v, ("row", "col"), pairs)

    def total(term):
        size = term.shape[0] // 2
        low, high = term[:size], term[size:]
        v = jnp.where(x == 0, low, high) + recv_holder(ox, jnp.where(x == 0, high, low))
        v = v + recv_holder(outer, v, mids)
        v = v + recv_holder(inner, v, mids)
        v = jnp.where((z == 0) | (z == 3), recv_holder(inner, v, ends), v)
        w = recv_holder(ox, v)
        term = jnp.where(x == 0, jnp.concatenate([v, w]), jnp.concatenate([w, v]))
        pairs = [(holder(i), other(i)) for i in range(ncol)]
        return jnp.where(is_holder, term, lax.ppermute(term, ("row", "col"), pairs))

    wanted = c % (ncol // 2)
    pick = sum(k * (wanted == p).astype(jnp.int32) for k, p in enumerate(planes))
    place = jnp.stack([x, pick])
    swap = lambda v: lax.ppermute(v, "row", [(0, 1), (1, 0)])
    shape = (ns, grid_rows, width)

    a0, b0 = lax.optimization_barrier((scale(0, 0, width), scale(1, 0, width)))
    ax0, a1, am = recv(ox, a0), recv(za, a0), recv(inner, a0, mids)
    b1, bx0 = recv(za, b0), recv(ox, b0)
    acc_a = add(None, (near[0], a0))
    acc_b = add(None, (near[0], b0))
    bm = recv(inner, after(b0, am), mids)
    square = jnp.stack([tdot(diag_inverse[i], diag_inverse[i], HIGHEST) for i in range(ns)])
    a1, ax0, am, acc_a, acc_b, square = lax.optimization_barrier(
        (a1, ax0, am, acc_a, acc_b, square)
    )
    ae, an, ax1 = recv(inner, am, ends), recv(inner, a1, mids), recv(ox, a1)
    bn = recv(inner, b1, mids)
    af = recv(inner, an, ends)
    acc_a = add(acc_a, (far[0], ax0), (near[1], a1))
    acc_b = add(acc_b, (far[0], bx0), (near[1], b1))
    a2 = am + ae
    ax2 = recv(ox, after(a2, acc_a))
    ax1, an, af, a2, bm, acc_a, acc_b = lax.optimization_barrier(
        (ax1, an, af, a2, bm, acc_a, acc_b)
    )
    a3 = an + af
    ax3 = recv(ox, a3)
    be, bf = recv(inner, bm, ends), recv(inner, bn, ends)
    acc_a = add(
        acc_a, (far[1], after(ax1, ax2)), (near[2], a2), (near[3], a3), (far[2], ax2), light=1000
    )
    b2 = after(bm + be, acc_a)
    bx2 = recv(ox, b2)
    acc_a = add(acc_a, (far[3], after(ax3, b2)), light=1000)
    got_a = swap(acc_a)
    bf, bn, bx0, bx2, acc_a = lax.optimization_barrier((bf, bn, bx0, bx2, acc_a))
    b3 = bn + bf
    bx1, bx3 = recv(za, bx0), recv(ox, b3)
    acc_b = add(acc_b, (near[2], b2), (near[3], b3), (far[2], bx2), light=1000)
    got_a = after(got_a, acc_b)
    full, term_a = finish(None, acc_a, got_a, place, (a0, a1, a2, a3), (ax0, ax1, ax2, ax3), shape, 0)
    acc_b = add(acc_b, (far[1], bx1), (far[3], after(bx3, term_a)))
    sum_a = total(term_a)
    got_b = swap(acc_b)
    full, term_b = finish(full, acc_b, got_b, place, (b0, b1, b2, b3), (bx0, bx1, bx2, bx3), shape, 1)
    return full, square - jnp.stack([sum_a, total(term_b)])


def plain_path(sigma_anc, factor_rows, diag_inverse, row_pattern, anc_pattern):
    nrow = lax.axis_size("row")
    ncol = lax.axis_size("col")
    r = lax.axis_index("row")
    c = lax.axis_index("col")
    own_rows = factor_rows.shape[1]
    grid_rows, grid_cols = sigma_anc.shape
    row_mask = jnp.repeat(row_pattern.astype(jnp.float32), BLK, axis=1)
    local = lax.dynamic_slice_in_dim(row_mask, (r * ncol + c) * own_rows, own_rows, 1)
    lower = factor_rows * local[:, :, None]
    scaled = jnp.einsum("sgb,sbc->sgc", lower, diag_inverse, precision=HIGHEST)
    piece = lax.all_gather(scaled, "col", axis=1, tiled=True)
    anc = jnp.repeat(anc_pattern.astype(jnp.float32), BLK, axis=0)
    anc = lax.dynamic_slice_in_dim(anc, c * grid_rows, grid_rows, 0)
    anc = jnp.repeat(anc, BLK, axis=1)
    anc = lax.dynamic_slice_in_dim(anc, r * grid_cols, grid_cols, 1)
    total = jnp.einsum("fg,sgc->sfc", sigma_anc * anc, piece, precision=HIGHEST)
    cross = -lax.psum(total, "row")
    half = c // (ncol // nrow)
    start = (c % (ncol // nrow)) * grid_rows
    mine = lax.dynamic_slice_in_dim(piece, start, grid_rows, 1)
    mine = jnp.where(r == half, mine, 0.0)
    term = jnp.einsum("sfc,sfd->scd", mine, cross, precision=HIGHEST)
    term = lax.psum(term, ("row", "col"))
    square = jnp.einsum("sbc,sbd->scd", diag_inverse, diag_inverse, precision=HIGHEST)
    return cross, square - term


def on_device(sigma_anc, factor_rows, diag_inverse, row_pattern, anc_pattern):
    own_rows, ncol = factor_rows.shape[1], lax.axis_size("col")
    fits = (
        ncol == 8
        and lax.axis_size("row") == 2
        and own_rows % BLK == 0
        and factor_rows.shape[0] == 2
        and sigma_anc.shape[0] % (3 * BLK) == 0
    )
    path = grid_path if fits else plain_path
    return path(sigma_anc, factor_rows, diag_inverse, row_pattern, anc_pattern)


def solution(mesh):
    in_specs = (
        P(("parts", "col"), "row"),
        P("parts", ("row", "col"), None),
        P("parts", None, None),
        P("parts", None),
        P("parts", None),
    )
    out_specs = (P("parts", "col", None), P("parts", None, None))
    return jax.shard_map(
        on_device, mesh=mesh, in_specs=in_specs, out_specs=out_specs, check_vma=False
    )
```
